512 devices in a mesh: dp: 8 (over x, core), row: 4 (over z_hi), col: 16 (over z_lo, y).
Axes of the slice: x: 4, y: 8, z: 8 (z_hi: 4, z_lo: 2; z = z_hi * 2 + z_lo), core: 2. Of those that a mesh axis runs over, the one named last changes fastest.
Arguments:
- activations: bfloat16 [2560, 12288], P(('dp', 'col'), 'row'), may hold values from -24 to 24
- out_grad: bfloat16 [2560, 6144], P(('dp', 'row'), 'col'), may hold values from -2 to 2
- qkv_weight: bfloat16 [12288, 6144], P('row', 'col'), may hold values from -0.0546875 to 0.0546875
Outputs:
- input_grad: bfloat16 [2560, 12288], P(('dp', 'col'), 'row')
- weight_grad: bfloat16 [12288, 6144], P('row', 'col')
The draws below stay inside these ranges and needn't reach their ends.
All inputs are finite; a program needn't handle non-finite values.
Results may differ from the reference program's by a relative error of at most 0.02.
Values may be sent and summed in bfloat16 or wider, within the bound.
No kernel may reach another device: no remote copies, remote signals or barrier semaphores. Data moves between devices by JAX's collectives and lax.ppermute only.
A program may use at most 64 MiB of HBM per device.

```python
import jax
import jax.numpy as jnp
from jax import lax

D = 12288
COLS = 6144
TOK_GROUP = 320
TOKENS = 2560
N_DP = 8
N_COL = 16


def spiked(array, rng, source, target, blocks, factor):
    owner, partner = [(jnp.arange(array.shape[position]) // (array.shape[position] // blocks)).reshape([-1 if axis == position else 1 for axis in range(array.ndim)]) for position in (source, target)]
    chosen = jax.random.permutation(rng, blocks)[partner]
    strong = (owner == chosen) | (owner == (partner + blocks // 2) % blocks)
    return jnp.where(strong, factor * array, array)


def steps_of(stream_key, dims, shards, low, top_value):
    def one(dim, shards_of):
        heights = jax.random.uniform(jax.random.fold_in(jax.random.fold_in(stream_key, 6), dim), (shards_of,), jnp.float32, low / len(shards), top_value / len(shards))
        return jnp.repeat(jnp.exp(heights), dims[dim] // shards_of).reshape((-1,) + (1,) * (len(dims) - dim - 1))

    gain = one(*shards[0])
    for cut in shards[1:]:
        gain = gain * one(*cut)
    return gain


def gaussian(stream_key, extent, spread, limit, cuts=(), kind=jnp.bfloat16):
    gain = steps_of(stream_key, extent, cuts, -0.22, 0.18) if cuts else 1.0
    values = jax.random.normal(stream_key, extent, jnp.float32) * spread * gain
    return jnp.minimum(jnp.maximum(values, -limit), limit).astype(kind)


def bell_draw_with(rng, shape, spread, reach, shards, heavy, kind=jnp.bfloat16):
    values = spread * jax.random.normal(rng, shape, jnp.float32)
    if shards:
        values = values * steps_of(rng, shape, shards, -0.22, 0.18)
    return jnp.clip(spiked(values, jax.random.fold_in(rng, 3), *heavy), -reach, reach).astype(kind)


def setup_inputs(seed: int = 0) -> dict:
    seeds = jax.random.split(jax.random.key(seed), 4)
    return {
        "activations": bell_draw_with(seeds[0], (TOKENS, D), 1.0, 24.0, ((0, 128), (1, 4)), (0, 1, 128, 5.5)),
        "out_grad": gaussian(seeds[1], (TOKENS, COLS), 0.3, 2.0, ((0, 32), (1, 16))),
        "qkv_weight": gaussian(seeds[2], (D, COLS), D ** -0.5, 0.0546875, ((0, 4), (1, 16))),
    }


def reference(activations, out_grad, qkv_weight):
    width = COLS // N_COL

    def column_block(total, index):
        grads = lax.dynamic_slice_in_dim(out_grad, index * width, width, 1)
        weights = lax.dynamic_slice_in_dim(qkv_weight, index * width, width, 1)
        part = lax.dot_general(grads, weights, (((1,), (1,)), ((), ())), preferred_element_type=jnp.float32)
        return total + part, None

    input_sum, _ = lax.scan(column_block, jnp.zeros((TOKENS, D), jnp.float32), jnp.arange(N_COL, dtype=jnp.int32))

    def group_block(total, index):
        inputs = lax.dynamic_slice_in_dim(activations, index * TOK_GROUP, TOK_GROUP, 0)
        grads = lax.dynamic_slice_in_dim(out_grad, index * TOK_GROUP, TOK_GROUP, 0)
        part = lax.dot_general(inputs, grads, (((0,), (0,)), ((), ())), preferred_element_type=jnp.float32)
        rounded = lax.optimization_barrier(part.astype(jnp.bfloat16))
        return total + rounded.astype(jnp.float32), None

    weight_sum, _ = lax.scan(group_block, jnp.zeros((D, COLS), jnp.float32), jnp.arange(N_DP, dtype=jnp.int32))
    return input_sum.astype(jnp.bfloat16), (weight_sum / N_DP).astype(jnp.bfloat16)
```

```python
import jax
import jax.numpy as jnp
from jax import lax
from jax.sharding import Mesh, PartitionSpec as P

F32 = jnp.float32
BF16 = jnp.bfloat16


def swap(value, axis):
    return lax.ppermute(value, axis, [(0, 1), (1, 0)])


def around(value, axis, step):
    size = lax.axis_size(axis)
    return lax.ppermute(value, axis, [(i, (i + step) % size) for i in range(size)])


def block(array, index, size):
    return lax.dynamic_slice_in_dim(array, index * size, size, 0)


def token_order(rows, zh, core):
    shape = (rows, rows)
    want = lax.broadcasted_iota(jnp.int32, shape, 0)
    have = lax.broadcasted_iota(jnp.int32, shape, 1)
    unit, inner = want // 20, want % 20
    y, zl, g = unit // 4, (unit // 2) % 2, unit % 2
    part = zl * 2 + y // 4
    source = ((g + core) % 2) * 320 + ((part - zh) % 4) * 80 + (y % 4) * 20 + inner
    return (source == have).astype(BF16)


def body(activations, out_grad, qkv_weight):
    x, core, zh, zl = (lax.axis_index(name) for name in ("x", "core", "zh", "zl"))
    ny = lax.axis_size("y")
    quarters = activations.reshape(20, 4, 768).transpose(1, 0, 2)
    mine = lax.all_to_all(quarters, ("zl", "core"), 0, 0, tiled=True).reshape(80, 768)
    acts = lax.all_to_all(
        jnp.broadcast_to(mine[None], (ny, 80, 768)), "y", 0, 0, tiled=True
    ).reshape(640, 768)
    grads = jnp.concatenate([out_grad, swap(out_grad, "zl")], axis=1)
    grads = jnp.concatenate([grads] + [around(grads, "zh", -k) for k in (1, 2, 3)], axis=0)
    grads = jnp.concatenate([grads, swap(grads, "core")], axis=0)
    grads = lax.dot_general(
        token_order(640, zh, core), grads, (((1,), (0,)), ((), ())), preferred_element_type=F32
    ).astype(BF16)
    weight = jnp.concatenate(
        [
            block(qkv_weight, zl * 2 + core, 768),
            swap(block(qkv_weight, (1 - zl) * 2 + core, 768), "zl"),
        ],
        axis=1,
    )
    parts = lax.dot_general(
        grads, weight, (((1,), (1,)), ((), ())), preferred_element_type=F32
    ).astype(BF16)
    parts = lax.all_to_all(parts.reshape(ny, 80, 768), "y", 0, 0, tiled=True)
    parts = parts.astype(F32).sum(0).astype(BF16)
    input_grad = lax.all_to_all(parts.reshape(4, 20, 768), ("zl", "core"), 0, 0, tiled=True)
    input_grad = input_grad.transpose(1, 0, 2).reshape(20, 3072)
    group = lax.dot_general(
        acts, grads, (((0,), (0,)), ((), ())), preferred_element_type=F32
    ).astype(BF16)
    total = block(group, x, 192).astype(F32)
    for k in (1, 2, 3):
        total += around(block(group, (x + k) % 4, 192), "x", k).astype(F32)
    total = (total / 8).astype(BF16)
    own, other = total[:, :384], total[:, 384:]
    pair = jnp.stack([jnp.where(zl == 0, own, other), jnp.where(zl == 0, other, own)])
    spread = jnp.broadcast_to(pair[None], (4, 2, 192, 384)).reshape(8, 192, 384)
    half = lax.all_to_all(spread, ("x", "zl"), 0, 0, tiled=True)
    half = half.reshape(4, 2, 192, 384).transpose(1, 0, 2, 3).reshape(2, 768, 384)
    other_half = swap(half, "core")
    first = jnp.where(core == 0, half, other_half)
    second = jnp.where(core == 0, other_half, half)
    weight_grad = jnp.stack([first, second], axis=1).reshape(3072, 384)
    return input_grad, weight_grad


def solution(mesh):
    fine = Mesh(mesh.devices.reshape(4, 2, 4, 2, 8), ("x", "core", "zh", "zl", "y"))
    tokens, grads, features = P(("x", "core", "zl", "y"), "zh"), P(("x", "core", "zh"), ("zl", "y")), P("zh", ("zl", "y"))
    return jax.shard_map(
        body,
        mesh=fine,
        in_specs=(tokens, grads, features),
        out_specs=(tokens, features),
        check_vma=False,
    )
```

```python
import jax
import jax.numpy as jnp
from jax import lax
from jax.experimental import pallas as pl
from jax.experimental.pallas import tpu as pltpu
from jax.sharding import Mesh, PartitionSpec as P

F32 = jnp.float32
BF16 = jnp.bfloat16
I32 = jnp.int32
UNIT = 20
ROWS = 4 * UNIT
QUARTER = 768


def swap(value, axis):
    return lax.ppermute(value, axis, [(0, 1), (1, 0)])


def around(value, axis, step):
    size = lax.axis_size(axis)
    return lax.ppermute(value, axis, [(i, (i + step) % size) for i in range(size)])


def after(value, *others):
    return lax.optimization_barrier((value,) + others)[0]


def block(array, index, size):
    return lax.dynamic_slice_in_dim(array, index * size, size, 0)


def order_kernel(own, other, weight_own, weight_other, grads, parts, gathered, pick):
    core, zh = lax.axis_index("core"), lax.axis_index("zh")
    half = own.shape[0]
    total = 2 * half
    gathered[:half] = own[...]
    gathered[half:] = other[...]
    row = lax.broadcasted_iota(I32, (ROWS, 1), 0)
    unit = sum((row >= UNIT * i).astype(I32) for i in (1, 2, 3))
    zl = (unit >= 2).astype(I32)
    group = unit - 2 * zl
    side = jnp.where(group == core, 0, half)
    column = lax.broadcasted_iota(I32, (ROWS, total), 1)
    for y in range(8):
        piece = (2 * zl + (y // 4) - zh + 4) & 3
        source = side + piece * ROWS + (y % 4) * UNIT + row - unit * UNIT
        pick[y * ROWS : (y + 1) * ROWS] = jnp.where(source == column, 1.0, 0.0).astype(BF16)

    @pl.loop(0, total // 160)
    def _(tile):
        rows = pl.ds(pl.multiple_of(tile * 160, 160), 160)
        ordered = jnp.dot(pick[rows], gathered[...], preferred_element_type=F32).astype(BF16)
        grads[rows] = ordered
        wide = ordered.shape[1] // 2
        contract = (((1,), (1,)), ((), ()))
        parts[rows] = (
            lax.dot_general(ordered[:, :wide], weight_own[...], contract, preferred_element_type=F32)
            + lax.dot_general(ordered[:, wide:], weight_other[...], contract, preferred_element_type=F32)
        ).astype(BF16)


def order_and_multiply(own, other, weight_own, weight_other):
    half, columns = own.shape
    full = jax.ShapeDtypeStruct((2 * half, columns), BF16)
    spec = pl.BlockSpec(memory_space=pltpu.VMEM)
    return pl.pallas_call(
        order_kernel,
        out_shape=(full, full),
        in_specs=[spec] * 4,
        out_specs=(spec, spec),
        scratch_shapes=[pltpu.VMEM((2 * half, columns), BF16), pltpu.VMEM((2 * half, 2 * half), BF16)],
        compiler_params=pltpu.CompilerParams(vmem_limit_bytes=24 * 2**20),
        cost_estimate=pl.CostEstimate(flops=1000, bytes_accessed=1000, transcendentals=0),
        name="order_and_multiply",
    )(own, other, weight_own, weight_other)


def body(activations, out_grad, qkv_weight):
    x, core, zh, zl = (lax.axis_index(name) for name in ("x", "core", "zh", "zl"))
    ny = lax.axis_size("y")
    near = jnp.concatenate([out_grad] + [around(out_grad, "zh", -k) for k in (1, 2, 3)], axis=0)
    quarters = activations.reshape(UNIT, 4, QUARTER).transpose(1, 0, 2)
    mine = lax.all_to_all(quarters, ("zl", "core"), 0, 0, tiled=True).reshape(ROWS, QUARTER)
    spread = after(jnp.broadcast_to(mine[None], (ny, ROWS, QUARTER)), near)
    acts = lax.all_to_all(spread, "y", 0, 0, tiled=True).reshape(ny * ROWS, QUARTER)
    grads = jnp.concatenate([near, swap(near, "zl")], axis=1)
    weight_own = block(qkv_weight, zl * 2 + core, QUARTER)
    weight_other = block(qkv_weight, (1 - zl) * 2 + core, QUARTER)
    weight_other = swap(after(weight_other, grads), "zl")
    grads, parts = order_and_multiply(grads, swap(grads, "core"), weight_own, weight_other)
    acts, grads = lax.optimization_barrier((acts, grads, parts))[:2]
    parts = lax.all_to_all(parts.reshape(ny, ROWS, QUARTER), "y", 0, 0, tiled=True)
    parts = parts.astype(F32).sum(0).astype(BF16).reshape(4, UNIT, QUARTER)
    group = lax.dot_general(
        acts, grads, (((0,), (0,)), ((), ())), preferred_element_type=F32
    ).astype(BF16)
    total = block(group, x, 192).astype(F32)
    for k in (1, 2, 3):
        total += around(block(group, (x + k) % 4, 192), "x", k).astype(F32)
    total = (total / 8).astype(BF16)
    own, other = total[:, :384], swap(total[:, 384:], "zl")
    pair = jnp.stack([jnp.where(zl == 0, own, other), jnp.where(zl == 0, other, own)])
    spread = jnp.broadcast_to(pair[None], (4, 2, 192, 384))
    half = lax.all_to_all(after(spread, parts), "x", 0, 0, tiled=True)
    half = half.transpose(1, 0, 2, 3).reshape(2, 768, 384)
    place = zl * 2 + core

    def piece(q):
        return lax.dynamic_index_in_dim(parts, q, 0, keepdims=False)

    relative = [
        piece(place),
        swap(piece(place ^ 1), "core"),
        swap(piece(place ^ 2), "zl"),
        lax.ppermute(piece(place ^ 3), ("core", "zl"), [(0, 3), (3, 0), (1, 2), (2, 1)]),
    ]
    relative = jnp.stack(relative)
    input_grad = jnp.concatenate(
        [lax.dynamic_index_in_dim(relative, place ^ q, 0, keepdims=False) for q in range(4)], axis=1
    )
    half = after(half, input_grad)
    other_half = swap(half, "core")
    first = jnp.where(core == 0, half, other_half)
    second = jnp.where(core == 0, other_half, half)
    weight_grad = jnp.stack([first, second], axis=1).reshape(3072, 384)
    return input_grad, weight_grad


def solution(mesh):
    fine = Mesh(mesh.devices.reshape(4, 2, 4, 2, 8), ("x", "core", "zh", "zl", "y"))
    tokens, features = P(("x", "core", "zl", "y"), "zh"), P("zh", ("zl", "y"))
    return jax.shard_map(
        body,
        mesh=fine,
        in_specs=(tokens, P(("x", "core", "zh"), ("zl", "y")), features),
        out_specs=(tokens, features),
        check_vma=False,
    )
```

```python
import jax
import jax.numpy as jnp
from jax import lax
from jax.experimental import pallas as pl
from jax.experimental.pallas import tpu as pltpu
from jax.sharding import Mesh, PartitionSpec as P

F32 = jnp.float32
BF16 = jnp.bfloat16
I32 = jnp.int32
UNIT = 20
PAIR = 2 * UNIT


def swap(value, axis):
    return lax.ppermute(value, axis, [(0, 1), (1, 0)])


def around(value, axis, step):
    size = lax.axis_size(axis)
    return lax.ppermute(value, axis, [(i, (i + step) % size) for i in range(size)])


def after(value, *others):
    return lax.optimization_barrier((value,) + others)[0]


def block(array, index, size):
    return lax.dynamic_slice_in_dim(array, index * size, size, 0)


def call(kernel, out_shape, in_spaces, out_spaces, scratch, name, flops=1000):
    return pl.pallas_call(
        kernel,
        out_shape=out_shape,
        in_specs=[pl.BlockSpec(memory_space=space) for space in in_spaces],
        out_specs=jax.tree.map(lambda space: pl.BlockSpec(memory_space=space), out_spaces),
        scratch_shapes=scratch,
        compiler_params=pltpu.CompilerParams(vmem_limit_bytes=10 * 2**20),
        cost_estimate=pl.CostEstimate(flops=flops, bytes_accessed=1000, transcendentals=0),
        name=name,
    )


def spread_kernel(rows, gate, out):
    for y in range(out.shape[0]):
        out[y] = rows[...]


def spread_out(rows, gate):
    return call(
        spread_kernel,
        jax.ShapeDtypeStruct((8,) + rows.shape, BF16),
        [pltpu.VMEM, pl.ANY],
        pltpu.VMEM,
        [],
        "spread",
    )(rows, gate)


def order_kernel(piece0, piece1, piece2, piece3, grads, gathered, pick):
    zh = lax.axis_index("zh")
    total = grads.shape[0]
    quarter = total // 4
    for k, piece in enumerate((piece0, piece1, piece2, piece3)):
        gathered[k * quarter : (k + 1) * quarter] = piece[...]
    row = lax.broadcasted_iota(I32, (PAIR, 1), 0)
    zl = (row >= UNIT).astype(I32)
    column = lax.broadcasted_iota(I32, (PAIR, total), 1)
    for y in range(8):
        piece = (2 * zl + (y // 4) - zh + 4) & 3
        source = piece * quarter + (y % 4) * UNIT + row - zl * UNIT
        pick[y * PAIR : (y + 1) * PAIR] = jnp.where(source == column, 1.0, 0.0)
    grads[...] = jnp.dot(
        pick[...].astype(BF16), gathered[...], preferred_element_type=F32
    ).astype(BF16)


def order(pieces):
    rows, columns = pieces[0].shape
    return call(
        order_kernel,
        jax.ShapeDtypeStruct((4 * rows, columns), BF16),
        [pltpu.VMEM] * 4,
        pltpu.VMEM,
        [pltpu.VMEM((4 * rows, columns), BF16), pltpu.VMEM((4 * rows, 4 * rows), F32)],
        "order",
    )(*pieces)


def multiply_kernel(near, other, weight, received, gate, parts, held, sem):
    rows, columns = received.shape
    first = (lax.axis_index("zl") * 2 + lax.axis_index("core")) * rows
    copy = pltpu.make_async_copy(weight.at[pl.ds(pl.multiple_of(first, rows), rows)], held, sem)
    copy.start()
    copy.wait()
    contract = (((1,), (1,)), ((), ()))
    tokens = near.shape[0]
    for group, grads in enumerate((near, other)):
        for tile in range(rows // 256):
            inner = slice(tile * 256, (tile + 1) * 256)
            parts[group * tokens : (group + 1) * tokens, inner] = (
                lax.dot_general(
                    grads[:, :columns], held[inner], contract, preferred_element_type=F32
                )
                + lax.dot_general(
                    grads[:, columns:], received[inner], contract, preferred_element_type=F32
                )
            ).astype(BF16)


def multiply(near, other, weight, received, gate):
    return call(
        multiply_kernel,
        jax.ShapeDtypeStruct((2 * near.shape[0], received.shape[0]), BF16),
        [pltpu.VMEM, pltpu.VMEM, pl.ANY, pltpu.VMEM, pl.ANY],
        pltpu.VMEM,
        [pltpu.VMEM(received.shape, BF16), pltpu.SemaphoreType.DMA],
        "multiply",
        3 * 10**9,
    )(near, other, weight, received, gate)


def outer_kernel(acts, near, other, own, send1, send2, send3, total):
    rows = near.shape[0]
    width = near.shape[1] // 3
    for tile in range(3):
        columns = slice(tile * width, (tile + 1) * width)
        total[:, columns] = sum(
            lax.dot_general(
                acts[k * rows : (k + 1) * rows],
                grads[:, columns],
                (((0,), (0,)), ((), ())),
                preferred_element_type=F32,
            )
            for k, grads in enumerate((near, other))
        )
    chunk = own.shape[0]
    x = lax.axis_index("x")
    for k, out in enumerate((own, send1, send2, send3)):
        start = pl.multiple_of(((x + k) & 3) * chunk, chunk)
        out[...] = total[pl.ds(start, chunk)].astype(out.dtype)


def outer(acts, near, other):
    features, columns = acts.shape[1], near.shape[1]
    shape = (features // 4, columns)
    return call(
        outer_kernel,
        (jax.ShapeDtypeStruct(shape, F32),) + (jax.ShapeDtypeStruct(shape, BF16),) * 3,
        [pltpu.VMEM] * 3,
        (pltpu.VMEM,) * 4,
        [pltpu.VMEM((features, columns), F32)],
        "outer",
    )(acts, near, other)


def combine_kernel(own, got1, got2, got3, near, far):
    columns = near.shape[1]
    total = own[...] + got1[...].astype(F32) + got2[...].astype(F32) + got3[...].astype(F32)
    total = (total * 0.125).astype(BF16)
    near[...] = total[:, :columns]
    far[...] = total[:, columns:]


def combine(own, got):
    half = jax.ShapeDtypeStruct((own.shape[0], own.shape[1] // 2), BF16)
    return call(
        combine_kernel, (half, half), [pltpu.VMEM] * 4, (pltpu.VMEM, pltpu.VMEM), [], "combine", 10**11
    )(own, *got)


def add_up_kernel(source, gate, total, parts, sem):
    copy = pltpu.make_async_copy(source, parts, sem)
    copy.start()
    copy.wait()
    sums = parts[0].astype(F32)
    for y in range(1, parts.shape[0]):
        sums += parts[y].astype(F32)
    total[...] = sums.astype(BF16)


def add_up(parts, gate):
    return call(
        add_up_kernel,
        jax.ShapeDtypeStruct(parts.shape[1:], BF16),
        [pltpu.HBM, pl.ANY],
        pltpu.VMEM,
        [pltpu.VMEM(parts.shape, BF16), pltpu.SemaphoreType.DMA],
        "add_up",
    )(parts, gate)


def stack_kernel(piece0, piece1, piece2, piece3, gate, out):
    for k, piece in enumerate((piece0, piece1, piece2, piece3)):
        out[k] = piece[...]


def stack(pieces, gate):
    return call(
        stack_kernel,
        jax.ShapeDtypeStruct((4,) + pieces[0].shape, BF16),
        [pltpu.VMEM] * 4 + [pl.ANY],
        pltpu.VMEM,
        [],
        "stack",
    )(*pieces, gate)


def place_kernel(near, next1, next2, next3, other, out, sems):
    x, core = lax.axis_index("x"), lax.axis_index("core")
    chunk = near.shape[1]
    copies = []
    for k, mine in enumerate((near, next1, next2, next3)):
        for zl in range(2):
            for far in range(2):
                half = 1 - core if far else core
                row = (((zl * 2 + half) * 4) + ((x - k + 4) & 3)) * chunk
                copies.append(
                    pltpu.make_async_copy(
                        other.at[k, zl] if far else mine.at[zl],
                        out.at[pl.ds(pl.multiple_of(row, chunk), chunk)],
                        sems.at[len(copies)],
                    )
                )
    for copy in copies:
        copy.start()
    for copy in copies:
        copy.wait()


def place(chunks, other):
    pairs, chunk, columns = chunks[0].shape
    return call(
        place_kernel,
        jax.ShapeDtypeStruct((16 * chunk, columns), BF16),
        [pltpu.VMEM] * 5,
        pltpu.HBM,
        [pltpu.SemaphoreType.DMA((16,))],
        "place",
    )(*chunks, other)


def body(activations, out_grad, qkv_weight):
    core, zl = lax.axis_index("core"), lax.axis_index("zl")
    features = qkv_weight.shape[0]
    quarter = features // 4
    quarters = activations.reshape(UNIT, 2, 2, quarter).transpose(2, 1, 0, 3)
    mine = lax.all_to_all(
        quarters.reshape(4, UNIT, quarter), ("core", "zl"), 0, 0, tiled=True
    ).reshape(2 * PAIR, quarter)
    beside = swap(out_grad, "zl")
    spread = spread_out(mine, beside)
    acts = lax.all_to_all(spread, "y", 0, 0, tiled=True).reshape(8, 2, PAIR, quarter)
    near = jnp.concatenate([out_grad, beside], axis=1)
    near = order([near] + [around(near, "zh", -k) for k in (1, 2, 3)])
    received = block(qkv_weight, (1 - zl) * 2 + core, quarter)
    received = swap(after(received, near), "zl")
    acts = jnp.concatenate(
        [
            lax.dynamic_index_in_dim(acts, core ^ c, 1, keepdims=False).reshape(8 * PAIR, quarter)
            for c in range(2)
        ],
        axis=0,
    )
    far = swap(near, "core")
    own, *sends = outer(acts, near, far)
    got = [around(send, "x", k + 1) for k, send in enumerate(sends)]
    parts = multiply(near, far, qkv_weight, received, far)
    parts = parts.reshape(2, 8, PAIR, quarter).transpose(1, 0, 2, 3)
    parts = lax.all_to_all(parts.reshape(8, 2 * PAIR, quarter), "y", 0, 0, tiled=True)
    own, other = combine(own, got)
    other = swap(other, "zl")
    pair = jnp.stack([jnp.where(zl == 0, own, other), jnp.where(zl == 0, other, own)])
    chunks = [pair] + [around(pair, "x", k) for k in (1, 2, 3)]
    total = add_up(parts, chunks[3])
    parts = total.reshape(2, 2, UNIT, quarter)
    parts = jnp.concatenate([block(parts, core ^ c, 1) for c in range(2)], axis=0)
    parts = lax.all_to_all(
        parts.reshape(4, UNIT, quarter), ("core", "zl"), 0, 0, tiled=True
    ).reshape(2, 2, UNIT, quarter)
    input_grad = parts.transpose(2, 1, 0, 3).reshape(UNIT, features)
    weight_grad = place(chunks, swap(stack(chunks, parts), "core"))
    return input_grad, weight_grad


def solution(mesh):
    fine = Mesh(mesh.devices.reshape(4, 2, 4, 2, 8), ("x", "core", "zh", "zl", "y"))
    tokens, features = P(("x", "core", "zl", "y"), "zh"), P("zh", ("zl", "y"))
    return jax.shard_map(
        body,
        mesh=fine,
        in_specs=(tokens, P(("x", "core", "zh"), ("zl", "y")), features),
        out_specs=(tokens, features),
        check_vma=False,
    )
```

```python
import jax
import jax.numpy as jnp
from jax import lax
from jax.experimental import pallas as pl
from jax.experimental.pallas import tpu as pltpu
from jax.sharding import Mesh, PartitionSpec as P

F32 = jnp.float32
BF16 = jnp.bfloat16
I32 = jnp.int32
UNIT = 20
PAIR = 2 * UNIT


def swap(value, axis):
    return lax.ppermute(value, axis, [(0, 1), (1, 0)])


def around(value, axis, step):
    size = lax.axis_size(axis)
    return lax.ppermute(value, axis, [(i, (i + step) % size) for i in range(size)])


def after(value, *others):
    return lax.optimization_barrier((value,) + others)[0]


def block(array, index, size):
    return lax.dynamic_slice_in_dim(array, index * size, size, 0)


def call(kernel, out_shape, in_spaces, out_spaces, scratch, name, flops=1000):
    return pl.pallas_call(
        kernel,
        out_shape=out_shape,
        in_specs=[pl.BlockSpec(memory_space=space) for space in in_spaces],
        out_specs=jax.tree.map(lambda space: pl.BlockSpec(memory_space=space), out_spaces),
        scratch_shapes=scratch,
        compiler_params=pltpu.CompilerParams(vmem_limit_bytes=10 * 2**20),
        cost_estimate=pl.CostEstimate(flops=flops, bytes_accessed=1000, transcendentals=0),
        name=name,
    )


def spread_kernel(rows, gate, out):
    for y in range(out.shape[0]):
        out[y] = rows[...]


def spread_out(rows, gate):
    return call(
        spread_kernel,
        jax.ShapeDtypeStruct((8,) + rows.shape, BF16),
        [pltpu.VMEM, pl.ANY],
        pltpu.VMEM,
        [],
        "spread",
    )(rows, gate)


def order_kernel(piece0, piece1, piece2, piece3, grads, gathered, pick):
    zh = lax.axis_index("zh")
    total = grads.shape[0]
    quarter = total // 4
    for k, piece in enumerate((piece0, piece1, piece2, piece3)):
        gathered[k * quarter : (k + 1) * quarter] = piece[...]
    row = lax.broadcasted_iota(I32, (PAIR, 1), 0)
    zl = (row >= UNIT).astype(I32)
    column = lax.broadcasted_iota(I32, (PAIR, total), 1)
    for y in range(8):
        piece = (2 * zl + (y // 4) - zh + 4) & 3
        source = piece * quarter + (y % 4) * UNIT + row - zl * UNIT
        pick[y * PAIR : (y + 1) * PAIR] = jnp.where(source == column, 1.0, 0.0)
    grads[...] = jnp.dot(
        pick[...].astype(BF16), gathered[...], preferred_element_type=F32
    ).astype(BF16)


def order(pieces):
    rows, columns = pieces[0].shape
    return call(
        order_kernel,
        jax.ShapeDtypeStruct((4 * rows, columns), BF16),
        [pltpu.VMEM] * 4,
        pltpu.VMEM,
        [pltpu.VMEM((4 * rows, columns), BF16), pltpu.VMEM((4 * rows, 4 * rows), F32)],
        "order",
    )(*pieces)


def cut_kernel(weight, gate, out, sem):
    rows = out.shape[0]
    first = ((1 - lax.axis_index("zl")) * 2 + lax.axis_index("core")) * rows
    copy = pltpu.make_async_copy(weight.at[pl.ds(pl.multiple_of(first, rows), rows)], out, sem)
    copy.start()
    copy.wait()


def cut(weight, gate):
    return call(
        cut_kernel,
        jax.ShapeDtypeStruct((weight.shape[0] // 4, weight.shape[1]), BF16),
        [pl.ANY, pl.ANY],
        pltpu.VMEM,
        [pltpu.SemaphoreType.DMA],
        "cut",
    )(weight, gate)


def multiply_kernel(near, other, weight, received, gate, parts, held, sem):
    rows, columns = received.shape
    first = (lax.axis_index("zl") * 2 + lax.axis_index("core")) * rows
    copy = pltpu.make_async_copy(weight.at[pl.ds(pl.multiple_of(first, rows), rows)], held, sem)
    copy.start()
    copy.wait()
    contract = (((1,), (1,)), ((), ()))
    tokens = near.shape[0]
    for group, grads in enumerate((near, other)):
        for tile in range(rows // 256):
            inner = slice(tile * 256, (tile + 1) * 256)
            parts[group * tokens : (group + 1) * tokens, inner] = (
                lax.dot_general(
                    grads[:, :columns], held[inner], contract, preferred_element_type=F32
                )
                + lax.dot_general(
                    grads[:, columns:], received[inner], contract, preferred_element_type=F32
                )
            ).astype(BF16)


def multiply(near, other, weight, received, gate):
    return call(
        multiply_kernel,
        jax.ShapeDtypeStruct((2 * near.shape[0], received.shape[0]), BF16),
        [pltpu.VMEM, pltpu.VMEM, pl.ANY, pltpu.VMEM, pl.ANY],
        pltpu.VMEM,
        [pltpu.VMEM(received.shape, BF16), pltpu.SemaphoreType.DMA],
        "multiply",
    )(near, other, weight, received, gate)


def outer_kernel(acts, near, other, own, send1, send2, send3, total):
    rows = near.shape[0]
    width = near.shape[1] // 3
    for tile in range(3):
        columns = slice(tile * width, (tile + 1) * width)
        total[:, columns] = sum(
            lax.dot_general(
                acts[k * rows : (k + 1) * rows],
                grads[:, columns],
                (((0,), (0,)), ((), ())),
                preferred_element_type=F32,
            )
            for k, grads in enumerate((near, other))
        )
    chunk = own.shape[0]
    x = lax.axis_index("x")
    for k, out in enumerate((own, send1, send2, send3)):
        start = pl.multiple_of(((x + k) & 3) * chunk, chunk)
        out[...] = total[pl.ds(start, chunk)].astype(out.dtype)


def outer(acts, near, other):
    features, columns = acts.shape[1], near.shape[1]
    shape = (features // 4, columns)
    return call(
        outer_kernel,
        (jax.ShapeDtypeStruct(shape, F32),) + (jax.ShapeDtypeStruct(shape, BF16),) * 3,
        [pltpu.VMEM] * 3,
        (pltpu.VMEM,) * 4,
        [pltpu.VMEM((features, columns), F32)],
        "outer",
    )(acts, near, other)


def combine_kernel(own, got1, got2, got3, near, far):
    columns = near.shape[1]
    total = own[...] + got1[...].astype(F32) + got2[...].astype(F32) + got3[...].astype(F32)
    total = (total * 0.125).astype(BF16)
    near[...] = total[:, :columns]
    far[...] = total[:, columns:]


def combine(own, got):
    half = jax.ShapeDtypeStruct((own.shape[0], own.shape[1] // 2), BF16)
    return call(
        combine_kernel, (half, half), [pltpu.VMEM] * 4, (pltpu.VMEM, pltpu.VMEM), [], "combine", 10**11
    )(own, *got)


def add_up_kernel(source, gate, total, parts, sem):
    copy = pltpu.make_async_copy(source, parts, sem)
    copy.start()
    copy.wait()
    sums = parts[0].astype(F32)
    for y in range(1, parts.shape[0]):
        sums += parts[y].astype(F32)
    total[...] = sums.astype(BF16)


def add_up(parts, gate):
    return call(
        add_up_kernel,
        jax.ShapeDtypeStruct(parts.shape[1:], BF16),
        [pltpu.HBM, pl.ANY],
        pltpu.VMEM,
        [pltpu.VMEM(parts.shape, BF16), pltpu.SemaphoreType.DMA],
        "add_up",
    )(parts, gate)


def stack_kernel(piece0, piece1, piece2, piece3, gate, out):
    for k, piece in enumerate((piece0, piece1, piece2, piece3)):
        out[k] = piece[...]


def stack(pieces, gate):
    return call(
        stack_kernel,
        jax.ShapeDtypeStruct((4,) + pieces[0].shape, BF16),
        [pltpu.VMEM] * 4 + [pl.ANY],
        pltpu.VMEM,
        [],
        "stack",
    )(*pieces, gate)


def place_kernel(near, next1, next2, next3, other, out, sems):
    x, core = lax.axis_index("x"), lax.axis_index("core")
    chunk = near.shape[1]
    copies = []
    for k, mine in enumerate((near, next1, next2, next3)):
        for zl in range(2):
            for far in range(2):
                half = 1 - core if far else core
                row = (((zl * 2 + half) * 4) + ((x - k + 4) & 3)) * chunk
                copies.append(
                    pltpu.make_async_copy(
                        other.at[k, zl] if far else mine.at[zl],
                        out.at[pl.ds(pl.multiple_of(row, chunk), chunk)],
                        sems.at[len(copies)],
                    )
                )
    for copy in copies:
        copy.start()
    for copy in copies:
        copy.wait()


def place(chunks, other):
    pairs, chunk, columns = chunks[0].shape
    return call(
        place_kernel,
        jax.ShapeDtypeStruct((16 * chunk, columns), BF16),
        [pltpu.VMEM] * 5,
        pltpu.HBM,
        [pltpu.SemaphoreType.DMA((16,))],
        "place",
    )(*chunks, other)


def body(activations, out_grad, qkv_weight):
    core, zl = lax.axis_index("core"), lax.axis_index("zl")
    features = qkv_weight.shape[0]
    quarter = features // 4
    quarters = activations.reshape(UNIT, 2, 2, quarter).transpose(2, 1, 0, 3)
    mine = lax.all_to_all(
        quarters.reshape(4, UNIT, quarter), ("core", "zl"), 0, 0, tiled=True
    ).reshape(2 * PAIR, quarter)
    beside = swap(out_grad, "zl")
    spread = spread_out(mine, beside)
    acts = lax.all_to_all(spread, "y", 0, 0, tiled=True).reshape(8, 2, PAIR, quarter)
    near = jnp.concatenate([out_grad, beside], axis=1)
    near = order([near] + [around(near, "zh", -k) for k in (1, 2, 3)])
    acts = jnp.concatenate(
        [
            lax.dynamic_index_in_dim(acts, core ^ c, 1, keepdims=False).reshape(8 * PAIR, quarter)
            for c in range(2)
        ],
        axis=0,
    )
    far = swap(near, "core")
    own, *sends = outer(acts, near, far)
    got = [around(send, "x", k + 1) for k, send in enumerate(sends)]
    received = swap(cut(qkv_weight, near), "zl")
    parts = multiply(near, far, qkv_weight, received, far)
    parts = parts.reshape(2, 8, PAIR, quarter).transpose(1, 0, 2, 3)
    parts = lax.all_to_all(parts.reshape(8, 2 * PAIR, quarter), "y", 0, 0, tiled=True)
    own, other = combine(own, got)
    other = swap(other, "zl")
    pair = jnp.stack([jnp.where(zl == 0, own, other), jnp.where(zl == 0, other, own)])
    chunks = [pair] + [around(pair, "x", k) for k in (1, 2, 3)]
    total = add_up(parts, chunks[3])
    parts = total.reshape(2, 2, UNIT, quarter)
    parts = jnp.concatenate([block(parts, core ^ c, 1) for c in range(2)], axis=0)
    parts = lax.all_to_all(
        parts.reshape(4, UNIT, quarter), ("core", "zl"), 0, 0, tiled=True
    ).reshape(2, 2, UNIT, quarter)
    input_grad = parts.transpose(2, 1, 0, 3).reshape(UNIT, features)
    weight_grad = place(chunks, swap(stack(chunks, input_grad), "core"))
    return input_grad, weight_grad


def solution(mesh):
    fine = Mesh(mesh.devices.reshape(4, 2, 4, 2, 8), ("x", "core", "zh", "zl", "y"))
    tokens, features = P(("x", "core", "zl", "y"), "zh"), P("zh", ("zl", "y"))
    return jax.shard_map(
        body,
        mesh=fine,
        in_specs=(tokens, P(("x", "core", "zh"), ("zl", "y")), features),
        out_specs=(tokens, features),
        check_vma=False,
    )
```

```python
import jax
import jax.numpy as jnp
from jax import lax
from jax.experimental import pallas as pl
from jax.experimental.pallas import tpu as pltpu
from jax.sharding import Mesh, PartitionSpec as P

F32 = jnp.float32
BF16 = jnp.bfloat16
I32 = jnp.int32
UNIT = 20
PAIR = 2 * UNIT


def swap(value, axis):
    return lax.ppermute(value, axis, [(0, 1), (1, 0)])


def around(value, axis, step):
    size = lax.axis_size(axis)
    return lax.ppermute(value, axis, [(i, (i + step) % size) for i in range(size)])


def after(value, *others):
    return lax.optimization_barrier((value,) + others)[0]


def block(array, index, size):
    return lax.dynamic_slice_in_dim(array, index * size, size, 0)


def call(kernel, out_shape, in_spaces, out_spaces, scratch, name, flops=1000):
    return pl.pallas_call(
        kernel,
        out_shape=out_shape,
        in_specs=[pl.BlockSpec(memory_space=space) for space in in_spaces],
        out_specs=jax.tree.map(lambda space: pl.BlockSpec(memory_space=space), out_spaces),
        scratch_shapes=scratch,
        compiler_params=pltpu.CompilerParams(vmem_limit_bytes=10 * 2**20),
        cost_estimate=pl.CostEstimate(flops=flops, bytes_accessed=1000, transcendentals=0),
        name=name,
    )


def spread_kernel(rows, gate, out):
    for y in range(out.shape[0]):
        out[y] = rows[...]


def spread_out(rows, gate):
    return call(
        spread_kernel,
        jax.ShapeDtypeStruct((8,) + rows.shape, BF16),
        [pltpu.VMEM, pl.ANY],
        pltpu.VMEM,
        [],
        "spread",
    )(rows, gate)


def order_kernel(piece0, piece1, piece2, piece3, grads, gathered, pick):
    zh = lax.axis_index("zh")
    total = grads.shape[0]
    quarter = total // 4
    for k, piece in enumerate((piece0, piece1, piece2, piece3)):
        gathered[k * quarter : (k + 1) * quarter] = piece[...]
    row = lax.broadcasted_iota(I32, (PAIR, 1), 0)
    zl = (row >= UNIT).astype(I32)
    column = lax.broadcasted_iota(I32, (PAIR, total), 1)
    for y in range(8):
        piece = (2 * zl + (y // 4) - zh + 4) & 3
        source = piece * quarter + (y % 4) * UNIT + row - zl * UNIT
        pick[y * PAIR : (y + 1) * PAIR] = jnp.where(source == column, 1.0, 0.0)
    grads[...] = jnp.dot(
        pick[...].astype(BF16), gathered[...], preferred_element_type=F32
    ).astype(BF16)


def order(pieces):
    rows, columns = pieces[0].shape
    return call(
        order_kernel,
        jax.ShapeDtypeStruct((4 * rows, columns), BF16),
        [pltpu.VMEM] * 4,
        pltpu.VMEM,
        [pltpu.VMEM((4 * rows, columns), BF16), pltpu.VMEM((4 * rows, 4 * rows), F32)],
        "order",
    )(*pieces)


def cut_kernel(weight, gate, out, sem):
    rows = out.shape[0]
    first = ((1 - lax.axis_index("zl")) * 2 + lax.axis_index("core")) * rows
    copy = pltpu.make_async_copy(weight.at[pl.ds(pl.multiple_of(first, rows), rows)], out, sem)
    copy.start()
    copy.wait()


def cut(weight, gate):
    return call(
        cut_kernel,
        jax.ShapeDtypeStruct((weight.shape[0] // 4, weight.shape[1]), BF16),
        [pl.ANY, pl.ANY],
        pltpu.VMEM,
        [pltpu.SemaphoreType.DMA],
        "cut",
    )(weight, gate)


def multiply_kernel(near, other, weight, received, gate, parts, held, sem):
    rows, columns = received.shape
    first = (lax.axis_index("zl") * 2 + lax.axis_index("core")) * rows
    copy = pltpu.make_async_copy(weight.at[pl.ds(pl.multiple_of(first, rows), rows)], held, sem)
    copy.start()
    copy.wait()
    contract = (((1,), (1,)), ((), ()))
    tokens = near.shape[0]
    for group, grads in enumerate((near, other)):
        for tile in range(rows // 256):
            inner = slice(tile * 256, (tile + 1) * 256)
            parts[group * tokens : (group + 1) * tokens, inner] = (
                lax.dot_general(
                    grads[:, :columns], held[inner], contract, preferred_element_type=F32
                )
                + lax.dot_general(
                    grads[:, columns:], received[inner], contract, preferred_element_type=F32
                )
            ).astype(BF16)


def multiply(near, other, weight, received, gate):
    return call(
        multiply_kernel,
        jax.ShapeDtypeStruct((2 * near.shape[0], received.shape[0]), BF16),
        [pltpu.VMEM, pltpu.VMEM, pl.ANY, pltpu.VMEM, pl.ANY],
        pltpu.VMEM,
        [pltpu.VMEM(received.shape, BF16), pltpu.SemaphoreType.DMA],
        "multiply",
    )(near, other, weight, received, gate)


def outer_kernel(acts, near, other, own, send1, send2, send3, total):
    rows = near.shape[0]
    width = near.shape[1] // 3
    for tile in range(3):
        columns = slice(tile * width, (tile + 1) * width)
        total[:, columns] = sum(
            lax.dot_general(
                acts[k * rows : (k + 1) * rows],
                grads[:, columns],
                (((0,), (0,)), ((), ())),
                preferred_element_type=F32,
            )
            for k, grads in enumerate((near, other))
        )
    chunk = own.shape[0]
    x = lax.axis_index("x")
    for k, out in enumerate((own, send1, send2, send3)):
        start = pl.multiple_of(((x + k) & 3) * chunk, chunk)
        out[...] = total[pl.ds(start, chunk)].astype(out.dtype)


def outer(acts, near, other):
    features, columns = acts.shape[1], near.shape[1]
    shape = (features // 4, columns)
    return call(
        outer_kernel,
        (jax.ShapeDtypeStruct(shape, F32),) + (jax.ShapeDtypeStruct(shape, BF16),) * 3,
        [pltpu.VMEM] * 3,
        (pltpu.VMEM,) * 4,
        [pltpu.VMEM((features, columns), F32)],
        "outer",
    )(acts, near, other)


def combine_kernel(own, got1, got2, got3, near, far):
    columns = near.shape[1]
    total = own[...] + got1[...].astype(F32) + got2[...].astype(F32) + got3[...].astype(F32)
    total = (total * 0.125).astype(BF16)
    near[...] = total[:, :columns]
    far[...] = total[:, columns:]


def combine(own, got):
    half = jax.ShapeDtypeStruct((own.shape[0], own.shape[1] // 2), BF16)
    return call(
        combine_kernel, (half, half), [pltpu.VMEM] * 4, (pltpu.VMEM, pltpu.VMEM), [], "combine"
    )(own, *got)


def pass_on_kernel(value, out):
    out[...] = value[...]


def pass_on(value):
    shape = jax.ShapeDtypeStruct(value.shape, value.dtype)
    return call(pass_on_kernel, shape, [pltpu.VMEM], pltpu.VMEM, [], "pass_on", 10**11)(value)


def add_up_kernel(source, gate, total, parts, sem):
    copy = pltpu.make_async_copy(source, parts, sem)
    copy.start()
    copy.wait()
    sums = parts[0].astype(F32)
    for y in range(1, parts.shape[0]):
        sums += parts[y].astype(F32)
    total[...] = sums.astype(BF16)


def add_up(parts, gate):
    return call(
        add_up_kernel,
        jax.ShapeDtypeStruct(parts.shape[1:], BF16),
        [pltpu.HBM, pl.ANY],
        pltpu.VMEM,
        [pltpu.VMEM(parts.shape, BF16), pltpu.SemaphoreType.DMA],
        "add_up",
    )(parts, gate)


def stack_kernel(piece0, piece1, piece2, piece3, gate, out):
    for k, piece in enumerate((piece0, piece1, piece2, piece3)):
        out[k] = piece[...]


def stack(pieces, gate):
    return call(
        stack_kernel,
        jax.ShapeDtypeStruct((4,) + pieces[0].shape, BF16),
        [pltpu.VMEM] * 4 + [pl.ANY],
        pltpu.VMEM,
        [],
        "stack",
    )(*pieces, gate)


def place_kernel(near, next1, next2, next3, other, out, sems):
    x, core = lax.axis_index("x"), lax.axis_index("core")
    chunk = near.shape[1]
    copies = []
    for k, mine in enumerate((near, next1, next2, next3)):
        for zl in range(2):
            for far in range(2):
                half = 1 - core if far else core
                row = (((zl * 2 + half) * 4) + ((x - k + 4) & 3)) * chunk
                copies.append(
                    pltpu.make_async_copy(
                        other.at[k, zl] if far else mine.at[zl],
                        out.at[pl.ds(pl.multiple_of(row, chunk), chunk)],
                        sems.at[len(copies)],
                    )
                )
    for copy in copies:
        copy.start()
    for copy in copies:
        copy.wait()


def place(chunks, other):
    pairs, chunk, columns = chunks[0].shape
    return call(
        place_kernel,
        jax.ShapeDtypeStruct((16 * chunk, columns), BF16),
        [pltpu.VMEM] * 5,
        pltpu.HBM,
        [pltpu.SemaphoreType.DMA((16,))],
        "place",
    )(*chunks, other)


def body(activations, out_grad, qkv_weight):
    core, zl = lax.axis_index("core"), lax.axis_index("zl")
    features = qkv_weight.shape[0]
    quarter = features // 4
    quarters = activations.reshape(UNIT, 2, 2, quarter).transpose(2, 1, 0, 3)
    mine = lax.all_to_all(
        quarters.reshape(4, UNIT, quarter), ("core", "zl"), 0, 0, tiled=True
    ).reshape(2 * PAIR, quarter)
    beside = swap(out_grad, "zl")
    spread = spread_out(mine, beside)
    acts = lax.all_to_all(spread, "y", 0, 0, tiled=True).reshape(8, 2, PAIR, quarter)
    near = jnp.concatenate([out_grad, beside], axis=1)
    near = order([near] + [around(near, "zh", -k) for k in (1, 2, 3)])
    acts = jnp.concatenate(
        [
            lax.dynamic_index_in_dim(acts, core ^ c, 1, keepdims=False).reshape(8 * PAIR, quarter)
            for c in range(2)
        ],
        axis=0,
    )
    far = swap(near, "core")
    own, *sends = outer(acts, near, far)
    got = [around(send, "x", k + 1) for k, send in enumerate(sends)]
    received = swap(cut(qkv_weight, near), "zl")
    parts = multiply(near, far, qkv_weight, received, far)
    parts = parts.reshape(2, 8, PAIR, quarter).transpose(1, 0, 2, 3)
    parts = lax.all_to_all(parts.reshape(8, 2 * PAIR, quarter), "y", 0, 0, tiled=True)
    own, other = combine(own, got)
    other = swap(pass_on(other), "zl")
    pair = jnp.stack([jnp.where(zl == 0, own, other), jnp.where(zl == 0, other, own)])
    chunks = [pair] + [around(pair, "x", k) for k in (1, 2, 3)]
    total = add_up(parts, chunks[3])
    parts = total.reshape(2, 2, UNIT, quarter)
    parts = jnp.concatenate([block(parts, core ^ c, 1) for c in range(2)], axis=0)
    parts = lax.all_to_all(
        parts.reshape(4, UNIT, quarter), ("core", "zl"), 0, 0, tiled=True
    ).reshape(2, 2, UNIT, quarter)
    input_grad = parts.transpose(2, 1, 0, 3).reshape(UNIT, features)
    weight_grad = place(chunks, swap(stack(chunks, input_grad), "core"))
    return input_grad, weight_grad


def solution(mesh):
    fine = Mesh(mesh.devices.reshape(4, 2, 4, 2, 8), ("x", "core", "zh", "zl", "y"))
    tokens, features = P(("x", "core", "zl", "y"), "zh"), P("zh", ("zl", "y"))
    return jax.shard_map(
        body,
        mesh=fine,
        in_specs=(tokens, P(("x", "core", "zh"), ("zl", "y")), features),
        out_specs=(tokens, features),
        check_vma=False,
    )
```
